32 devices in a mesh: enc: 4 (over x, core), fsdp: 8 (over z, y).
Axes of the slice: x: 2, y: 2, z: 4, core: 2. Of those that a mesh axis runs over, the one named last changes fastest.
Arguments:
- enc_features: bfloat16 [8, 8, 1024, 512], P(None, 'enc', 'fsdp'), may hold values from -6 to 6
- enc_gain: float32 [1, 512], replicated, may hold values from 0.1 to 1.9
- enc_kernel: bfloat16 [1, 3, 512, 512], replicated, may hold values from -0.15625 to 0.15625
- out_kernel: bfloat16 [512, 16], replicated, may hold values from -0.25 to 0.25
- clip_start: int32 [8], replicated, may hold values from 0 to 3
- assign: int32 [8], replicated, may hold values from 0 to 7, each once
- embed_weight: bfloat16 [3072, 64], P('fsdp'), may hold values from -0.75 to 0.75
- mod_shift: float32 [8, 3072], P('fsdp'), may hold values from -3 to 3
- mod_scale: float32 [8, 3072], P('fsdp'), may hold values from -3 to 3
- value_weight: bfloat16 [3072, 1536], P('fsdp'), may hold values from -0.109375 to 0.109375
- value_cotangent: bfloat16 [8, 8, 256, 1536], P('fsdp', 'enc'), may hold values from -6 to 6
Outputs:
- values: bfloat16 [8, 8, 256, 1536], P('fsdp', 'enc')
- grad_value: float32 [3072, 1536], P(('enc', 'fsdp'))
- grad_embed: float32 [3072, 64], P(('enc', 'fsdp'))
The draws below stay inside these ranges and needn't reach their ends.
Inputs may be any that keep to these rules, and one draw needn't show every extreme that they name: Sample s is made from clip assign[s]; every clip is taken by exactly one sample.
All inputs are finite; a program needn't handle non-finite values.
Results may differ from the reference program's by a relative error of at most 0.025.
Values may be sent and summed in bfloat16 or wider, within the bound.
A program may use at most 192 MiB of HBM per device.

```python
import jax
import jax.numpy as jnp
from jax import lax

D = 3072
C = 512
LAT = 16
L_ENC = 1
CLIPS = 8
FRAMES = 8
PATCHES = 256
PIX = 1024
HALF = 1536


def with_ends(values, own_key, least, high):
    longest = values.shape.index(max(values.shape))
    spots = []
    for shift in (0, 1):
        where = [jax.random.randint(jax.random.fold_in(own_key, axis), (), 0, length) for axis, length in enumerate(values.shape)]
        where[longest] = (where[longest] + shift) % values.shape[longest]
        spots.append(tuple(where))
    return values.at[spots[0]].set(least).at[spots[1]].set(high)


def block_scale(rng, extent, cuts, least, high):
    def one(dim, shards_of):
        draws = jax.random.uniform(jax.random.fold_in(jax.random.fold_in(rng, 6), dim), (shards_of,), jnp.float32, least / len(cuts), high / len(cuts))
        return jnp.repeat(jnp.exp(draws), extent[dim] // shards_of).reshape((-1,) + (1,) * (len(extent) - dim - 1))

    level = one(*cuts[0])
    for cut in cuts[1:]:
        level = level * one(*cut)
    return level


def gaussian(own_key, extent, width, limit, shards=(), kind=jnp.bfloat16):
    entries = jax.random.normal(own_key, extent, jnp.float32) * width
    if len(shards) > 0:
        entries = block_scale(own_key, extent, shards, -0.22, 0.18) * entries
    return jnp.clip(entries, min=-limit, max=limit).astype(kind)


def setup_inputs(seed: int = 0) -> dict:
    seeds = jax.random.split(jax.random.key(seed), 12)
    return {
        "enc_features": gaussian(seeds[0], (CLIPS, FRAMES, PIX, C), 1.0, 6.0, ((1, 4), (2, 8))),
        "enc_gain": jnp.clip(1.0 + 0.18 * jax.random.normal(seeds[1], (L_ENC, C), jnp.float32), 0.1, 1.9),
        "enc_kernel": gaussian(seeds[2], (L_ENC, 3, C, C), (3 * C) ** -0.5, 0.15625),
        "out_kernel": gaussian(seeds[3], (C, LAT), C ** -0.5, 0.25),
        "clip_start": with_ends(jax.random.randint(seeds[4], (CLIPS,), 0, FRAMES // 2), jax.random.fold_in(seeds[4], 1), 0, (FRAMES // 2) - 1).astype(jnp.int32),
        "assign": jax.random.permutation(seeds[5], CLIPS).astype(jnp.int32),
        "embed_weight": gaussian(seeds[6], (D, 4 * LAT), (4 * LAT) ** -0.5, 0.75, ((0, 8),)),
        "mod_shift": gaussian(seeds[7], (CLIPS, D), 0.5, 3.0, ((0, 8),), jnp.float32),
        "mod_scale": gaussian(seeds[8], (CLIPS, D), 0.5, 3.0, ((0, 8),), jnp.float32),
        "value_weight": gaussian(seeds[9], (D, HALF), D ** -0.5, 0.109375, ((0, 8),)),
        "value_cotangent": gaussian(seeds[10], (CLIPS, FRAMES, PATCHES, HALF), 1.0, 6.0, ((0, 8), (1, 4))),
    }


def encode_clip(features, start_frame, enc_gain, enc_kernel, out_kernel):
    frame_count = features.shape[0]
    live_mask = (jnp.arange(frame_count, dtype=jnp.int32) >= start_frame).astype(jnp.float32)[:, None, None]
    stored = features
    for layer_index in range(L_ENC):
        activation = stored.astype(jnp.float32)
        scaling = lax.rsqrt(lax.optimization_barrier(jnp.mean(activation * activation, axis=-1, keepdims=True)) + 1e-06)
        normed = (live_mask * activation * scaling * enc_gain[layer_index]).astype(jnp.bfloat16)
        padded = jnp.concatenate([jnp.zeros((2,) + normed.shape[1:], jnp.bfloat16), normed], axis=0)
        convolved = jnp.zeros(activation.shape, jnp.float32)
        for offset in range(3):
            window = padded[offset:offset + frame_count].reshape(-1, C)
            convolved = convolved + jnp.dot(window, enc_kernel[layer_index, offset], preferred_element_type=jnp.float32).reshape(activation.shape)
        stored = lax.optimization_barrier((activation + jax.nn.silu(convolved)).astype(jnp.bfloat16))
    latent = jnp.dot(stored.reshape(-1, C), out_kernel, preferred_element_type=jnp.float32).reshape(frame_count, PIX, LAT)
    latent = (latent * live_mask).astype(jnp.bfloat16)
    return latent.reshape(frame_count, PATCHES, 4 * LAT)

def reference(enc_features, enc_gain, enc_kernel, out_kernel, clip_start, assign, embed_weight, mod_shift, mod_scale, value_weight, value_cotangent):

    def encode_one(inputs_pair):
        return encode_clip(inputs_pair[0], inputs_pair[1], enc_gain, enc_kernel, out_kernel)
    latents = lax.map(encode_one, (enc_features, clip_start))
    samples = jnp.take(latents, assign.astype(jnp.int32), axis=0)

    def sample_step(carry, inputs_tuple):
        grad_w_sum, grad_e_sum = carry
        patch_block, shift_row, scale_row, cot_block = inputs_tuple
        token_rows = patch_block.reshape(-1, 4 * LAT)
        mixed = jnp.dot(token_rows, embed_weight.T, preferred_element_type=jnp.float32)
        row_mean = lax.optimization_barrier(jnp.mean(mixed, axis=-1, keepdims=True))
        centred = mixed - row_mean
        row_var = lax.optimization_barrier(jnp.mean(centred * centred, axis=-1, keepdims=True))
        inv_std = lax.rsqrt(row_var + 1e-06)
        unit = centred * inv_std
        modulated = (unit * (1.0 + scale_row) + shift_row).astype(jnp.bfloat16)
        projected = jnp.dot(modulated, value_weight, preferred_element_type=jnp.float32).astype(jnp.bfloat16)
        cot_rows = cot_block.reshape(-1, HALF)
        grad_w = jnp.dot(modulated.T, cot_rows, preferred_element_type=jnp.float32)
        grad_mod = jnp.dot(cot_rows, value_weight.T, preferred_element_type=jnp.float32)
        grad_unit = grad_mod * (1.0 + scale_row)
        grad_mixed = inv_std * (grad_unit - lax.optimization_barrier(jnp.mean(grad_unit, axis=-1, keepdims=True)) - unit * lax.optimization_barrier(jnp.mean(grad_unit * unit, axis=-1, keepdims=True)))
        grad_bf = grad_mixed.astype(jnp.bfloat16)
        grad_e = jnp.dot(grad_bf.T, token_rows, preferred_element_type=jnp.float32)
        return ((grad_w_sum + grad_w, grad_e_sum + grad_e), projected.reshape(cot_block.shape))
    start_carry = (jnp.zeros((D, HALF), jnp.float32), jnp.zeros((D, 4 * LAT), jnp.float32))
    (grad_value, grad_embed), values = lax.scan(sample_step, start_carry, (samples, mod_shift, mod_scale, value_cotangent))
    return (values, grad_value, grad_embed)
```

```python
import functools

import jax
import jax.numpy as jnp
from jax import lax
from jax.experimental import pallas as pl
from jax.experimental.pallas import tpu as pltpu
from jax.sharding import PartitionSpec as P

MESH = pl.DeviceIdType.MESH
F32, BF16 = jnp.float32, jnp.bfloat16
HIGH = lax.Precision.HIGHEST
VMEM = pl.BlockSpec(memory_space=pltpu.VMEM)
TAIL = 16


def dot(a, b, dims=((1,), (0,)), precision=None):
    return lax.dot_general(a, b, (dims, ((), ())), preferred_element_type=F32, precision=precision)


def meet(axes):
    barrier = pltpu.get_barrier_semaphore()
    total = 0
    for axis in axes:
        me, size = lax.axis_index(axis), lax.axis_size(axis)
        for k in range(1, size):
            pl.semaphore_signal(barrier, inc=1, device_id={axis: lax.rem(me + k, size)}, device_id_type=MESH)
        total += size - 1
    pl.semaphore_wait(barrier, total)


def spread(axis, source, target, sems):
    me, size = lax.axis_index(axis), lax.axis_size(axis)
    copies = []
    for k in range(1, size):
        peer = lax.rem(me + k, size)
        copy = pltpu.make_async_remote_copy(
            src_ref=source(peer), dst_ref=target(me),
            send_sem=sems.at[0, k - 1], recv_sem=sems.at[1, k - 1],
            device_id={axis: peer}, device_id_type=MESH)
        copy.start()
        copies.append(copy)
    return copies


def wait_all(copies):
    for copy in copies:
        copy.wait()


def prep_kernel(n_e, n_f, depth, embed_t, embed, weight, mod, full, gram, mod_all, weight_rows, embed_rows,
                part, landed, quarter, gsend, gland, mod_sems, gram_sems, part_sems, full_sems, row_sems):
    e, f = lax.axis_index("enc"), lax.axis_index("fsdp")
    width = embed_t.shape[0]
    rows = weight.shape[0]
    cols = weight.shape[1] // n_e
    block = rows // n_e
    mine = pl.ds(pl.multiple_of(e * cols, 128), cols)
    meet(("enc", "fsdp"))
    mod_copies = spread("fsdp", lambda peer: mod.at[peer], lambda me: mod_all.at[me], mod_sems)
    flat = embed_t[...]
    square = dot(flat, flat, ((1,), (1,)))
    total = jnp.sum(flat.astype(F32), axis=1, keepdims=True)
    gsend[...] = jnp.concatenate([square, jnp.broadcast_to(total, (width, width))], axis=1)
    gram_copies = spread("fsdp", lambda peer: gsend, lambda me: gland.at[me], gram_sems)
    mod_all[f] = mod[f]
    gland[f] = gsend[...]
    wait_all(mod_copies)
    wait_all(gram_copies)
    both = jnp.sum(gland[...], axis=0) * (1.0 / depth)
    mean = both[:, width:]
    mean_row = jnp.sum(mean * (lax.broadcasted_iota(jnp.int32, mean.shape, 0)
                               == lax.broadcasted_iota(jnp.int32, mean.shape, 1)).astype(F32), axis=0, keepdims=True)
    gram[...] = jnp.concatenate([both[:, :width] - mean * mean_row, mean], axis=1)
    centred = flat.astype(F32) - mean[:, :1]
    own = weight[:, mine]
    row_id = lax.broadcasted_iota(jnp.int32, (TAIL, rows), 0)
    for s in range(n_f):
        scale = 1.0 + mod_all[s, 0:1, :]
        shift = mod_all[s, 1:2, :]
        tail = jnp.where(row_id == 0, scale, jnp.where(row_id == 1, shift, 0.0))
        left = jnp.concatenate([centred * scale, tail], axis=0).astype(BF16)
        part[s] = dot(left, own).astype(BF16)
    part_copies = spread("fsdp", lambda peer: part.at[peer], lambda me: landed.at[me], part_sems)
    landed[f] = part[f]
    for k in range(n_e):
        where = n_e * f + k
        target, slot = lax.rem(where, n_f), where // n_f
        there = pl.ds(pl.multiple_of(slot * block, 16), block)
        here = pl.ds(k * block, block)

        def pair(make, slot=slot, there=there, here=here):
            return (make(weight.at[here, mine], weight_rows.at[there, :], slot, 0),
                    make(embed.at[here, :], embed_rows.at[there, :], slot, 1))

        @pl.when(target != f)
        def _(k=k, target=target, pair=pair):
            for copy in pair(lambda src, dst, slot, which: pltpu.make_async_remote_copy(
                    src_ref=src, dst_ref=dst, send_sem=row_sems.at[0, which, k], recv_sem=row_sems.at[1, which, slot],
                    device_id={"fsdp": target}, device_id_type=MESH)):
                copy.start()

        @pl.when(target == f)
        def _(k=k, pair=pair):
            for copy in pair(lambda src, dst, slot, which: pltpu.make_async_copy(src, dst, row_sems.at[0, which, k])):
                copy.start()
                copy.wait()

    wait_all(part_copies)
    quarter[...] = jnp.sum(landed[...].astype(F32), axis=0).astype(BF16)
    full_copies = spread("enc", lambda peer: quarter, lambda me: full.at[me], full_sems)
    full[e] = quarter[...]
    for k in range(n_e):
        where = n_e * f + k
        target = lax.rem(where, n_f)

        @pl.when(target != f)
        def _(k=k, target=target):
            here = pl.ds(k * block, block)
            for src, dst, which in ((weight.at[here, mine], weight_rows.at[here, :], 0), (embed.at[here, :], embed_rows.at[here, :], 1)):
                pltpu.make_async_remote_copy(
                    src_ref=src, dst_ref=dst, send_sem=row_sems.at[0, which, k], recv_sem=row_sems.at[1, which, k],
                    device_id={"fsdp": target}, device_id_type=MESH).wait_send()

    for slot in range(n_e):
        origin = (n_f * slot + f) // n_e

        @pl.when(origin != f)
        def _(slot=slot, origin=origin):
            here = pl.ds(slot * block, block)
            for src, dst, which in ((weight.at[here, mine], weight_rows.at[here, :], 0), (embed.at[here, :], embed_rows.at[here, :], 1)):
                pltpu.make_async_remote_copy(
                    src_ref=src, dst_ref=dst, send_sem=row_sems.at[0, which, slot], recv_sem=row_sems.at[1, which, slot],
                    device_id={"fsdp": origin}, device_id_type=MESH).wait_recv()

    wait_all(full_copies)


def encode_kernel(frames, assign, start, first, now, past, gain, taps, out_kernel, patches):
    s = pl.program_id(0)
    clip_start = start[assign[s]]
    pixels = now.shape[2]
    gains = gain[0:1, :]

    def norm(frame, frame_id):
        value = frame.astype(F32)
        live = jnp.where((frame_id >= clip_start) & (frame_id >= 0), 1.0, 0.0)
        scaling = lax.rsqrt(jnp.mean(value * value, axis=-1, keepdims=True) + 1e-06) * live
        return (value * scaling * gains).astype(BF16)

    base = first[0]
    normed = [norm(past[0, past.shape[1] - 2 + i], base - 2 + i) for i in range(2)]
    normed += [norm(now[0, i], base + i) for i in range(frames)]
    row = lax.broadcasted_iota(jnp.int32, (pixels, 4 * 16), 0)
    col = lax.broadcasted_iota(jnp.int32, (pixels, 4 * 16), 1)
    keep = lax.rem(row, 4) == col // 16
    pick = (lax.broadcasted_iota(jnp.int32, (pixels // 4, pixels), 0)
            == lax.broadcasted_iota(jnp.int32, (pixels // 4, pixels), 1) // 4).astype(BF16)
    left = jnp.concatenate([jnp.concatenate(normed[i:i + 3], axis=1) for i in range(frames)], axis=0)
    convolved = dot(left, taps[...])
    activation = jnp.concatenate([now[0, i] for i in range(frames)], axis=0).astype(F32)
    stored = (activation + convolved / (1.0 + jnp.exp(-convolved))).astype(BF16)
    latent = dot(stored, out_kernel[...])
    found = []
    for i in range(frames):
        live = jnp.where(base + i >= clip_start, 1.0, 0.0)
        wide = jnp.where(keep, latent[i * pixels:(i + 1) * pixels] * live, 0.0).astype(BF16)
        found.append(dot(pick, wide))
    patches[0] = jnp.concatenate(found, axis=0).astype(BF16)


def token_kernel(n_e, n_f, frames, depth, lat, full, gram, cot, mod_all, weight_rows, embed_rows,
                 values, grad_value, grad_embed,
                 tokens, left, qsend, qland, qsum, qall, rsend, rland, rsum, rall, vsend, vland, gsend, gland,
                 lat_sems, q_sems, r_sems, qa_sems, ra_sems, v_sems, g_sems):
    e, f = lax.axis_index("enc"), lax.axis_index("fsdp")
    width = lat.shape[2]
    each = lat.shape[1] // frames
    cols = full.shape[2]
    block = grad_value.shape[0]
    slim = width // n_e
    rows = weight_rows.shape[0]
    meet(("enc", "fsdp"))
    lat_copies = spread("fsdp", lambda peer: lat.at[peer], lambda me: tokens.at[me], lat_sems)
    tokens[f] = lat[f]
    unit_id = (lax.broadcasted_iota(jnp.int32, (width, width), 0)
               == lax.broadcasted_iota(jnp.int32, (width, width), 1)).astype(BF16)
    mean = gram[:, width:width + 1]
    centred = dot(unit_id, embed_rows[...], ((1,), (1,))) - mean
    row_id = lax.broadcasted_iota(jnp.int32, (TAIL, rows), 0)
    for s in range(n_f):
        tail = jnp.where(row_id == 0, mod_all[s, 3:4, :], 0.0)
        left[s] = jnp.concatenate([centred * (1.0 + mod_all[s, 2:3, :]), tail], axis=0).astype(BF16)
    wait_all(lat_copies)
    came = tokens[...].astype(F32)
    flat = jnp.concatenate(
        [came[:, i * each:(i + 1) * each, :].reshape(n_f * each, width) for i in range(frames)], axis=0)
    low = flat.astype(BF16)
    var = jnp.sum(flat * dot(flat, gram[:, :width], precision=HIGH), axis=1, keepdims=True)
    inv_std = lax.rsqrt(jnp.maximum(var, 0.0) + 1e-06)
    scaled = flat * inv_std
    count = flat.shape[0]
    ones = (lax.broadcasted_iota(jnp.int32, (count, width), 1) == 0).astype(F32)
    wide = jnp.concatenate([scaled, ones], axis=1).astype(BF16)
    dots = jnp.zeros((count, 1), F32)
    for i in range(n_e):
        here = slice(i * cols, (i + 1) * cols)
        factor = full[i]
        product = dot(low, factor[:width]) * inv_std
        values[:, here] = (product + factor[width:width + TAIL].astype(F32)[1:2]).astype(BF16)
        cot_part = cot[:, here]
        dots += jnp.sum(product * cot_part.astype(F32), axis=1, keepdims=True)
        qsend[i] = dot(wide, cot_part, ((0,), (0,)))[:width + TAIL].astype(BF16)
    q_copies = spread("enc", lambda peer: qsend.at[peer], lambda me: qland.at[me], q_sems)
    weighted = scaled * (inv_std * dots * (1.0 / depth))
    pairs = dot(weighted.astype(BF16), low, ((0,), (0,)))
    pairs = jnp.concatenate([pairs, jnp.zeros((width, width), F32)], axis=1)
    for i in range(n_e):
        rsend[i] = pairs[i * slim:(i + 1) * slim]
    r_copies = spread("enc", lambda peer: rsend.at[peer], lambda me: rland.at[me], r_sems)
    qland[e] = qsend[e]
    rland[e] = rsend[e]
    wait_all(q_copies)
    summed = jnp.sum(qland[...].astype(F32), axis=0)
    low_sum = summed.astype(BF16)
    qsum[...] = low_sum
    qall[f] = low_sum
    qa_copies = spread("fsdp", lambda peer: qsum, lambda me: qall.at[me], qa_sems)
    wait_all(r_copies)
    head = jnp.sum(rland[...], axis=0)
    ends = full[e][width:width + TAIL]
    drift = dot(ends, low_sum[:width], ((1,), (1,)))[:8] * (1.0 / depth)
    drift = jnp.where(lax.broadcasted_iota(jnp.int32, drift.shape, 0) == 0, drift, 0.0)
    both = jnp.concatenate([head, jnp.concatenate([drift, jnp.zeros_like(drift)], axis=1)], axis=0)
    rsum[...] = both
    rall[f] = both
    ra_copies = spread("fsdp", lambda peer: rsum, lambda me: rall.at[me], ra_sems)
    wait_all(qa_copies)
    every = qall[...].reshape(n_f * (width + TAIL), cols)
    lefts = left[...].reshape(n_f * (width + TAIL), rows)
    gradient = dot(lefts, every, ((0,), (0,)))
    for i in range(n_e):
        vsend[i] = gradient[i * block:(i + 1) * block].astype(BF16)
    v_copies = spread("enc", lambda peer: vsend.at[peer], lambda me: vland.at[me], v_sems)
    vland[e] = vsend[e]
    back = dot(every, weight_rows[...], ((1,), (1,)))
    total = jnp.zeros((width, rows), F32)
    for s in range(n_f):
        start = s * (width + TAIL)
        total += back[start:start + width] * (1.0 + mod_all[s, 2:3, :])
    wait_all(ra_copies)
    fix = jnp.sum(rall[...], axis=0)[:, :width]
    chosen = (lax.broadcasted_iota(jnp.int32, (slim + 8, width), 1)
              == lax.broadcasted_iota(jnp.int32, (slim + 8, width), 0) + e * slim) & (
                  lax.broadcasted_iota(jnp.int32, (slim + 8, width), 0) < slim)
    against = dot(chosen.astype(F32), centred, precision=HIGH)
    against = jnp.where(lax.broadcasted_iota(jnp.int32, against.shape, 0) == slim, 1.0, against)
    total -= dot(fix, against, ((0,), (0,)), precision=HIGH)
    turned = dot(total.astype(BF16), unit_id, ((0,), (0,)))
    turned = jnp.concatenate([turned, jnp.zeros_like(turned)], axis=1).astype(BF16)
    for i in range(n_e):
        gsend[i] = turned[i * block:(i + 1) * block]
    g_copies = spread("enc", lambda peer: gsend.at[peer], lambda me: gland.at[me], g_sems)
    gland[e] = gsend[e]
    wait_all(v_copies)
    for i in range(n_e):
        grad_value[:, i * cols:(i + 1) * cols] = vland[i].astype(F32)
    wait_all(g_copies)
    grad_embed[...] = jnp.sum(gland[...].astype(F32), axis=0)[:, :width]


def local(
    n_e,
    n_f,
    enc_features,
    enc_gain,
    enc_kernel,
    out_kernel,
    clip_start,
    assign,
    embed_weight,
    mod_shift,
    mod_scale,
    value_weight,
    value_cotangent,
):
    clips, frames, pixels, channels = enc_features.shape
    rows, half = value_weight.shape
    width = embed_weight.shape[1]
    depth, cols, block = rows * n_f, half // n_e, rows // n_e
    size = width + TAIL
    tokens = frames * value_cotangent.shape[2]
    shape = jax.ShapeDtypeStruct
    dma = lambda *n: pltpu.SemaphoreType.DMA(n)
    big = 56 * 1024 * 1024

    past = lax.ppermute(enc_features[:, frames - 2:], "enc", [(i, i + 1) for i in range(n_e - 1)])

    by_rows = lambda m: m.reshape(n_f, 1, rows)
    by_block = lambda m: m.reshape(n_e, n_f, block).transpose(1, 0, 2).reshape(n_f, 1, rows)
    mod = jnp.concatenate([by_rows(mod_scale), by_rows(mod_shift), by_block(mod_scale), by_block(mod_shift)], axis=1)
    full, gram, mod_all, weight_rows, embed_rows = pl.pallas_call(
        functools.partial(prep_kernel, n_e, n_f, depth),
        out_shape=(shape((n_e, size, cols), BF16), shape((width, 2 * width), F32), shape((n_f, 4, rows), F32),
                   shape((rows, cols), BF16), shape((rows, width), BF16)),
        in_specs=[VMEM] * 4, out_specs=(VMEM,) * 5,
        scratch_shapes=[
            pltpu.VMEM((n_f, size, cols), BF16), pltpu.VMEM((n_f, size, cols), BF16), pltpu.VMEM((size, cols), BF16),
            pltpu.VMEM((width, 2 * width), F32), pltpu.VMEM((n_f, width, 2 * width), F32),
            dma(2, n_f - 1), dma(2, n_f - 1), dma(2, n_f - 1), dma(2, n_e - 1), dma(2, 2, n_e)],
        compiler_params=pltpu.CompilerParams(collective_id=0, has_side_effects=True, vmem_limit_bytes=big),
        name="prepare",
    )(embed_weight.T, embed_weight, value_weight, mod)

    first = (lax.axis_index("enc") * frames).astype(jnp.int32).reshape(1)
    taps = enc_kernel.reshape(3 * channels, channels)
    spec = lambda shape, fn: pl.BlockSpec(shape, fn)
    fixed = lambda *shape: pl.BlockSpec(shape, lambda s, *_: (0,) * len(shape))
    lat = pl.pallas_call(
        functools.partial(encode_kernel, frames),
        out_shape=shape((clips, frames * pixels // 4, width), BF16),
        grid_spec=pltpu.PrefetchScalarGridSpec(
            num_scalar_prefetch=3, grid=(clips,),
            in_specs=[
                spec((1, frames, pixels, channels), lambda s, a, *_: (a[s], 0, 0, 0)),
                spec((1, 2, pixels, channels), lambda s, a, *_: (a[s], 0, 0, 0)),
                fixed(1, channels), fixed(3 * channels, channels), fixed(channels, width)],
            out_specs=spec((1, frames * pixels // 4, width), lambda s, *_: (s, 0, 0))),
        compiler_params=pltpu.CompilerParams(vmem_limit_bytes=big),
        name="encode",
    )(assign, clip_start, first, enc_features, past, enc_gain, taps, jnp.tile(out_kernel, (1, 4)))

    values, grad_value, grad_embed = pl.pallas_call(
        functools.partial(token_kernel, n_e, n_f, frames, depth),
        out_shape=(shape((tokens, half), BF16), shape((block, half), F32), shape((block, width), F32)),
        in_specs=[VMEM] * 7, out_specs=(VMEM,) * 3,
        scratch_shapes=[
            pltpu.VMEM((n_f, lat.shape[1], width), BF16), pltpu.VMEM((n_f, size, rows), BF16),
            pltpu.VMEM((n_e, size, cols), BF16), pltpu.VMEM((n_e, size, cols), BF16),
            pltpu.VMEM((size, cols), BF16), pltpu.VMEM((n_f, size, cols), BF16),
            pltpu.VMEM((n_e, width // n_e, 2 * width), F32), pltpu.VMEM((n_e, width // n_e, 2 * width), F32),
            pltpu.VMEM((width // n_e + 8, 2 * width), F32), pltpu.VMEM((n_f, width // n_e + 8, 2 * width), F32),
            pltpu.VMEM((n_e, block, cols), BF16), pltpu.VMEM((n_e, block, cols), BF16),
            pltpu.VMEM((n_e, block, 2 * width), BF16), pltpu.VMEM((n_e, block, 2 * width), BF16),
            dma(2, n_f - 1), dma(2, n_e - 1), dma(2, n_e - 1), dma(2, n_f - 1), dma(2, n_f - 1),
            dma(2, n_e - 1), dma(2, n_e - 1)],
        compiler_params=pltpu.CompilerParams(collective_id=1, has_side_effects=True, vmem_limit_bytes=big),
        name="tokens",
    )(lat, full, gram, value_cotangent.reshape(tokens, half), mod_all, weight_rows, embed_rows)
    return (values.reshape(value_cotangent.shape), grad_value, grad_embed)


def solution(mesh):
    in_specs = (
        P(None, "enc", "fsdp", None),
        P(),
        P(),
        P(),
        P(),
        P(),
        P("fsdp", None),
        P("fsdp", None),
        P("fsdp", None),
        P("fsdp", None),
        P("fsdp", "enc", None, None),
    )
    out_specs = (P("fsdp", "enc", None, None), P(("enc", "fsdp"), None), P(("enc", "fsdp"), None))
    body = functools.partial(local, mesh.shape["enc"], mesh.shape["fsdp"])
    return jax.shard_map(body, mesh=mesh, in_specs=in_specs, out_specs=out_specs, check_vma=False)
```

```python
import functools

import jax
import jax.numpy as jnp
from jax import lax
from jax.experimental import pallas as pl
from jax.experimental.pallas import tpu as pltpu
from jax.sharding import PartitionSpec as P

MESH = pl.DeviceIdType.MESH
F32, BF16 = jnp.float32, jnp.bfloat16
HIGH = lax.Precision.HIGHEST
VMEM = pl.BlockSpec(memory_space=pltpu.VMEM)
TAIL = 16


def dot(a, b, dims=((1,), (0,)), precision=None):
    return lax.dot_general(a, b, (dims, ((), ())), preferred_element_type=F32, precision=precision)


def meet(axes):
    barrier = pltpu.get_barrier_semaphore()
    total = 0
    for axis in axes:
        me, size = lax.axis_index(axis), lax.axis_size(axis)
        for k in range(1, size):
            pl.semaphore_signal(barrier, inc=1, device_id={axis: lax.rem(me + k, size)}, device_id_type=MESH)
        total += size - 1
    pl.semaphore_wait(barrier, total)


def spread(axis, source, target, sems):
    me, size = lax.axis_index(axis), lax.axis_size(axis)
    copies = []
    for k in range(1, size):
        peer = lax.rem(me + k, size)
        copy = pltpu.make_async_remote_copy(
            src_ref=source(peer), dst_ref=target(me),
            send_sem=sems.at[0, k - 1], recv_sem=sems.at[1, k - 1],
            device_id={axis: peer}, device_id_type=MESH)
        copy.start()
        copies.append(copy)
    return copies


def wait_all(copies):
    for copy in copies:
        copy.wait()


def program_kernel(n_e, n_f, frames, depth, start, assign, feat_hbm, gain, taps_hbm, out_t, embed_t, scale_row, shift_row,
                   weight, cot_hbm, values, grad_value, grad_embed,
                   feat, past, taps, own, cot, found, lat, tokens,
                   mod, mod_all, gsum, gram_all, part, landed, quarter, full, rows_out, rows_in, weight_rows,
                   left, staged, qsend, qland, qsum, qall, rsend, rland, rsum, rall, vsend, vland, gsend, gland,
                   load_sems, out_sems, halo_sems, mod_sems, gram_sems, part_sems, full_sems, row_sems,
                   lat_sems, q_sems, r_sems, qa_sems, ra_sems, v_sems, g_sems):
    e, f = lax.axis_index("enc"), lax.axis_index("fsdp")
    clips, _, pixels, channels = feat.shape
    width, rows = embed_t.shape
    cols = own.shape[2]
    block = rows // n_e
    slim = width // n_e
    each = pixels // 4
    mine = pl.ds(pl.multiple_of(e * cols, 128), cols)
    loads = [pltpu.make_async_copy(src, dst, load_sems.at[i]) for i, (src, dst) in enumerate(
        [(weight.at[:, :, mine], own), (feat_hbm, feat), (taps_hbm, taps), (cot_hbm, cot)])]
    for copy in loads:
        copy.start()
    for s in range(n_f):
        here = slice(s * rows, (s + 1) * rows)
        mod[s] = jnp.concatenate([scale_row[:, here], shift_row[:, here]], axis=0)
    flat = embed_t[...]
    square = dot(flat, flat, ((1,), (1,)))
    total = jnp.sum(flat.astype(F32), axis=1, keepdims=True)
    gsum[...] = jnp.concatenate([square, jnp.broadcast_to(total, (width, width))], axis=1)
    meet(("enc", "fsdp"))

    def halo(c, peer):
        return pltpu.make_async_remote_copy(
            src_ref=feat_hbm.at[c, pl.ds(frames - 2, 2)], dst_ref=past.at[c],
            send_sem=halo_sems.at[0, c], recv_sem=halo_sems.at[1, c],
            device_id={"enc": lax.rem(peer, n_e)}, device_id_type=MESH)

    mod_copies = spread("fsdp", lambda peer: mod.at[peer], lambda me: mod_all.at[me], mod_sems)
    gram_copies = spread("fsdp", lambda peer: gsum, lambda me: gram_all.at[me], gram_sems)

    @pl.when(e < n_e - 1)
    def _():
        @pl.loop(0, clips)
        def _(c):
            halo(c, e + 1).start()

    @pl.when(e == 0)
    def _():
        past[...] = jnp.zeros_like(past)

    def row_target(k):
        where = n_e * f + k
        return lax.rem(where, n_f), where // n_f

    def row_copy(which, k, slot, target=None):
        src = rows_out.at[k] if which else weight.at[k, :, mine]
        dst = (rows_in if which else weight_rows).at[slot]
        if target is None:
            return pltpu.make_async_copy(src, dst, row_sems.at[0, which, k])
        return pltpu.make_async_remote_copy(
            src_ref=src, dst_ref=dst, send_sem=row_sems.at[0, which, k], recv_sem=row_sems.at[1, which, slot],
            device_id={"fsdp": target}, device_id_type=MESH)

    def send_rows(which):
        for k in range(n_e):
            target, slot = row_target(k)

            @pl.when(target != f)
            def _(k=k, target=target, slot=slot):
                row_copy(which, k, slot, target).start()

            @pl.when(target == f)
            def _(k=k, target=target, slot=slot):
                inside = row_copy(which, k, slot)
                inside.start()
                inside.wait()

    send_rows(0)
    mod_all[f] = mod[f]
    gram_all[f] = gsum[...]
    wait_all(mod_copies)
    wait_all(gram_copies)
    both = jnp.sum(gram_all[...], axis=0) * (1.0 / depth)
    mean = both[:, width:]
    diagonal = (lax.broadcasted_iota(jnp.int32, mean.shape, 0) == lax.broadcasted_iota(jnp.int32, mean.shape, 1))
    gram = both[:, :width] - mean * jnp.sum(mean * diagonal.astype(F32), axis=0, keepdims=True)
    mean = mean[:, :1]
    unit_id = diagonal.astype(BF16)
    centred = flat.astype(F32) - mean
    loads[0].wait()
    own_flat = own[...].astype(F32).reshape(rows, cols).astype(BF16)
    row_id = lax.broadcasted_iota(jnp.int32, (TAIL, rows), 0)
    for s in range(n_f):
        scale = 1.0 + mod_all[s, 0:1, :]
        tail = jnp.where(row_id == 0, scale, jnp.where(row_id == 1, mod_all[s, 1:2, :], 0.0))
        factor = jnp.concatenate([centred * scale, tail], axis=0).astype(BF16)
        part[s] = dot(factor, own_flat).astype(BF16)
    part_copies = spread("fsdp", lambda peer: part.at[peer], lambda me: landed.at[me], part_sems)
    landed[f] = part[f]
    stack = [flat.astype(F32)] + [mod_all[s, 0:1, :] for s in range(n_f)] + [mod_all[s, 1:2, :] for s in range(n_f)]
    spare = rows_out.shape[2] - width - 2 * n_f
    if spare:
        stack.append(jnp.zeros((spare, rows), F32))
    rows_out[...] = jnp.concatenate(stack, axis=0).T.reshape(rows_out.shape)
    send_rows(1)

    gains = gain[0:1, :]
    base = e * frames
    row = lax.broadcasted_iota(jnp.int32, (pixels, width), 0)
    col = lax.broadcasted_iota(jnp.int32, (pixels, width), 1)
    keep = lax.rem(row, 4) == col // (width // 4)
    pick = (lax.broadcasted_iota(jnp.int32, (each, pixels), 0)
            == lax.broadcasted_iota(jnp.int32, (each, pixels), 1) // 4).astype(BF16)
    out_wide = jnp.concatenate([out_t[...]] * 4, axis=0)

    def encode(c, _):
        clip_start = start[c]

        @pl.when(e > 0)
        def _():
            halo(c, e + n_e - 1).wait_recv()

        def norm(frame, frame_id):
            value = frame.astype(F32)
            live = jnp.where((frame_id >= clip_start) & (frame_id >= 0), 1.0, 0.0)
            scaling = lax.rsqrt(jnp.mean(value * value, axis=-1, keepdims=True) + 1e-06) * live
            return (value * scaling * gains).astype(BF16)

        normed = [norm(past[c, i], base - 2 + i) for i in range(2)]
        normed += [norm(feat[c, i], base + i) for i in range(frames)]
        window = jnp.concatenate([jnp.concatenate(normed[i:i + 3], axis=1) for i in range(frames)], axis=0)
        convolved = dot(window, taps[...])
        activation = jnp.concatenate([feat[c, i] for i in range(frames)], axis=0).astype(F32)
        stored = (activation + convolved / (1.0 + jnp.exp(-convolved))).astype(BF16)
        latent = dot(stored, out_wide, ((1,), (1,)))
        picked = []
        for i in range(frames):
            live = jnp.where(base + i >= clip_start, 1.0, 0.0)
            picked.append(dot(pick, jnp.where(keep, latent[i * pixels:(i + 1) * pixels] * live, 0.0).astype(BF16)))
        found[c] = jnp.concatenate(picked, axis=0).astype(BF16)
        return 0

    loads[1].wait()
    loads[2].wait()
    cut = clips // 2
    lax.fori_loop(0, cut, encode, 0)
    wait_all(part_copies)
    quarter[...] = jnp.sum(landed[...].astype(F32), axis=0).astype(BF16)
    full_copies = spread("enc", lambda peer: quarter, lambda me: full.at[me], full_sems)
    full[e] = quarter[...]
    for which in range(2):
        for k in range(n_e):
            target, slot = row_target(k)

            @pl.when(target != f)
            def _(which=which, k=k, target=target, slot=slot):
                row_copy(which, k, slot, target).wait_send()

        for slot in range(n_e):
            origin = (n_f * slot + f) // n_e

            @pl.when(origin != f)
            def _(which=which, slot=slot, origin=origin):
                row_copy(which, slot, slot, origin).wait_recv()

    turned_in = rows_in[...].reshape(rows, rows_in.shape[2]).T
    weight_flat = weight_rows[...].astype(F32).reshape(rows, cols).astype(BF16)
    centred = turned_in[:width] - mean
    for s in range(n_f):
        tail = jnp.where(row_id == 0, turned_in[width + n_f + s:width + n_f + s + 1], 0.0)
        left[s] = jnp.concatenate([centred * (1.0 + turned_in[width + s:width + s + 1]), tail], axis=0).astype(BF16)
    lax.fori_loop(cut, clips, encode, 0)
    for s in range(n_f):
        lat[s] = found[assign[s]]
    lat_copies = spread("fsdp", lambda peer: lat.at[peer], lambda me: tokens.at[me], lat_sems)
    tokens[f] = lat[f]
    wait_all(full_copies)
    loads[3].wait()
    wait_all(lat_copies)
    came = tokens[...].astype(F32)
    flat = jnp.concatenate(
        [came[:, i * each:(i + 1) * each, :].reshape(n_f * each, width) for i in range(frames)], axis=0)
    low = flat.astype(BF16)
    var = jnp.sum(flat * dot(flat, gram, precision=HIGH), axis=1, keepdims=True)
    inv_std = lax.rsqrt(jnp.maximum(var, 0.0) + 1e-06)
    scaled = flat * inv_std
    count = flat.shape[0]
    ones = (lax.broadcasted_iota(jnp.int32, (count, width), 1) == 0).astype(F32)
    wide = jnp.concatenate([scaled, ones], axis=1).astype(BF16)
    dots = jnp.zeros((count, 1), F32)
    out_copies = []
    for i in range(n_e):
        here = slice(i * cols, (i + 1) * cols)
        factor = full[i]
        product = dot(low, factor[:width]) * inv_std
        staged[i] = (product + factor[width:width + TAIL].astype(F32)[1:2]).astype(BF16)
        out_copies.append(pltpu.make_async_copy(staged.at[i], values.at[:, pl.ds(i * cols, cols)], out_sems.at[i]))
        out_copies[-1].start()
        cot_part = cot[:, here]
        dots += jnp.sum(product * cot_part.astype(F32), axis=1, keepdims=True)
        qsend[i] = dot(wide, cot_part, ((0,), (0,)))[:width + TAIL].astype(BF16)
    q_copies = spread("enc", lambda peer: qsend.at[peer], lambda me: qland.at[me], q_sems)
    weighted = scaled * (inv_std * dots * (1.0 / depth))
    pairs = dot(weighted.astype(BF16), low, ((0,), (0,)))
    pairs = jnp.concatenate([pairs, jnp.zeros((width, width), F32)], axis=1)
    for i in range(n_e):
        rsend[i] = pairs[i * slim:(i + 1) * slim]
    r_copies = spread("enc", lambda peer: rsend.at[peer], lambda me: rland.at[me], r_sems)
    qland[e] = qsend[e]
    rland[e] = rsend[e]
    wait_all(q_copies)
    summed = jnp.sum(qland[...].astype(F32), axis=0)
    low_sum = summed.astype(BF16)
    qsum[...] = low_sum
    qall[f] = low_sum
    qa_copies = spread("fsdp", lambda peer: qsum, lambda me: qall.at[me], qa_sems)
    wait_all(r_copies)
    head = jnp.sum(rland[...], axis=0)
    ends = full[e][width:width + TAIL]
    drift = dot(ends, low_sum[:width], ((1,), (1,)))[:8] * (1.0 / depth)
    drift = jnp.where(lax.broadcasted_iota(jnp.int32, drift.shape, 0) == 0, drift, 0.0)
    both = jnp.concatenate([head, jnp.concatenate([drift, jnp.zeros_like(drift)], axis=1)], axis=0)
    rsum[...] = both
    rall[f] = both
    ra_copies = spread("fsdp", lambda peer: rsum, lambda me: rall.at[me], ra_sems)
    wait_all(qa_copies)
    every = qall[...].reshape(n_f * (width + TAIL), cols)
    lefts = left[...].reshape(n_f * (width + TAIL), rows)
    gradient = dot(lefts, every, ((0,), (0,)))
    for i in range(n_e):
        vsend[i] = gradient[i * block:(i + 1) * block].astype(BF16)
    v_copies = spread("enc", lambda peer: vsend.at[peer], lambda me: vland.at[me], v_sems)
    vland[e] = vsend[e]
    back = dot(every, weight_flat, ((1,), (1,)))
    total = jnp.zeros((width, rows), F32)
    for s in range(n_f):
        start = s * (width + TAIL)
        total += back[start:start + width] * (1.0 + turned_in[width + s:width + s + 1])
    wait_all(ra_copies)
    fix = jnp.sum(rall[...], axis=0)[:, :width]
    chosen = (lax.broadcasted_iota(jnp.int32, (slim + 8, width), 1)
              == lax.broadcasted_iota(jnp.int32, (slim + 8, width), 0) + e * slim) & (
                  lax.broadcasted_iota(jnp.int32, (slim + 8, width), 0) < slim)
    against = dot(chosen.astype(F32), centred, precision=HIGH)
    against = jnp.where(lax.broadcasted_iota(jnp.int32, against.shape, 0) == slim, 1.0, against)
    total -= dot(fix, against, ((0,), (0,)), precision=HIGH)
    turned = dot(total.astype(BF16), unit_id, ((0,), (0,)))
    turned = jnp.concatenate([turned, jnp.zeros_like(turned)], axis=1).astype(BF16)
    for i in range(n_e):
        gsend[i] = turned[i * block:(i + 1) * block]
    g_copies = spread("enc", lambda peer: gsend.at[peer], lambda me: gland.at[me], g_sems)
    gland[e] = gsend[e]
    wait_all(v_copies)
    for i in range(n_e):
        grad_value[:, i * cols:(i + 1) * cols] = vland[i].astype(F32)
    wait_all(g_copies)
    grad_embed[...] = jnp.sum(gland[...].astype(F32), axis=0)[:, :width]
    wait_all(out_copies)

    @pl.when(e < n_e - 1)
    def _():
        @pl.loop(0, clips)
        def _(c):
            halo(c, e + 1).wait_send()


def local(
    n_e,
    n_f,
    enc_features,
    enc_gain,
    enc_kernel,
    out_kernel,
    clip_start,
    assign,
    embed_weight,
    mod_shift,
    mod_scale,
    value_weight,
    value_cotangent,
):
    clips, frames, pixels, channels = enc_features.shape
    rows, half = value_weight.shape
    width = embed_weight.shape[1]
    depth, cols, block = rows * n_f, half // n_e, rows // n_e
    size = width + TAIL
    slim = width // n_e
    count = frames * value_cotangent.shape[2]
    lanes = -(-(width + 2 * n_f) // 128) * 128
    shape = jax.ShapeDtypeStruct
    dma = lambda *n: pltpu.SemaphoreType.DMA(n)
    b16 = lambda *n: pltpu.VMEM(n, BF16)
    f32 = lambda *n: pltpu.VMEM(n, F32)
    scalars = pl.BlockSpec(memory_space=pltpu.SMEM)
    far = pl.BlockSpec(memory_space=pl.ANY)
    patches = frames * pixels // 4
    values, grad_value, grad_embed = pl.pallas_call(
        functools.partial(program_kernel, n_e, n_f, frames, depth),
        out_shape=(shape((count, half), BF16), shape((block, half), F32), shape((block, width), F32)),
        in_specs=[scalars, scalars, far, VMEM, far, VMEM, VMEM, VMEM, VMEM, far, far],
        out_specs=(far, VMEM, VMEM),
        scratch_shapes=[
            b16(clips, frames, pixels, channels), b16(clips, 2, pixels, channels), b16(3 * channels, channels),
            b16(n_e, block, cols), b16(count, half), b16(clips, patches, width), b16(n_f, patches, width),
            b16(n_f, patches, width),
            f32(n_f, 2, rows), f32(n_f, 2, rows), f32(width, 2 * width), f32(n_f, width, 2 * width),
            b16(n_f, size, cols), b16(n_f, size, cols), b16(size, cols), b16(n_e, size, cols),
            f32(n_e, block, lanes), f32(n_e, block, lanes), b16(n_e, block, cols),
            b16(n_f, size, rows), b16(n_e, count, cols),
            b16(n_e, size, cols), b16(n_e, size, cols), b16(size, cols), b16(n_f, size, cols),
            f32(n_e, slim, 2 * width), f32(n_e, slim, 2 * width), f32(slim + 8, 2 * width), f32(n_f, slim + 8, 2 * width),
            b16(n_e, block, cols), b16(n_e, block, cols), b16(n_e, block, 2 * width), b16(n_e, block, 2 * width),
            dma(4), dma(n_e), dma(2, clips), dma(2, n_f - 1), dma(2, n_f - 1), dma(2, n_f - 1), dma(2, n_e - 1),
            dma(2, 2, n_e),
            dma(2, n_f - 1), dma(2, n_e - 1), dma(2, n_e - 1), dma(2, n_f - 1), dma(2, n_f - 1),
            dma(2, n_e - 1), dma(2, n_e - 1)],
        compiler_params=pltpu.CompilerParams(
            collective_id=0, has_side_effects=True, vmem_limit_bytes=56 * 1024 * 1024),
        name="program",
    )(clip_start, assign, enc_features, enc_gain, enc_kernel.reshape(3 * channels, channels), out_kernel.T,
      embed_weight.T, mod_scale, mod_shift, value_weight.reshape(n_e, block, half), value_cotangent.reshape(count, half))
    return (values.reshape(value_cotangent.shape), grad_value, grad_embed)


def solution(mesh):
    in_specs = (
        P(None, "enc", "fsdp", None),
        P(),
        P(),
        P(),
        P(),
        P(),
        P("fsdp", None),
        P("fsdp", None),
        P("fsdp", None),
        P("fsdp", None),
        P("fsdp", "enc", None, None),
    )
    out_specs = (P("fsdp", "enc", None, None), P(("enc", "fsdp"), None), P(("enc", "fsdp"), None))
    body = functools.partial(local, mesh.shape["enc"], mesh.shape["fsdp"])
    return jax.shard_map(body, mesh=mesh, in_specs=in_specs, out_specs=out_specs, check_vma=False)
```

```python
import functools

import jax
import jax.numpy as jnp
from jax import lax
from jax.experimental import pallas as pl
from jax.experimental.pallas import tpu as pltpu
from jax.sharding import PartitionSpec as P

MESH = pl.DeviceIdType.MESH
F32, BF16 = jnp.float32, jnp.bfloat16
HIGH = lax.Precision.HIGHEST
VMEM = pl.BlockSpec(memory_space=pltpu.VMEM)
TAIL = 16


def dot(a, b, dims=((1,), (0,)), precision=None):
    return lax.dot_general(a, b, (dims, ((), ())), preferred_element_type=F32, precision=precision)


def meet(axes):
    barrier = pltpu.get_barrier_semaphore()
    total = 0
    for axis in axes:
        me, size = lax.axis_index(axis), lax.axis_size(axis)
        for k in range(1, size):
            pl.semaphore_signal(barrier, inc=1, device_id={axis: lax.rem(me + k, size)}, device_id_type=MESH)
        total += size - 1
    pl.semaphore_wait(barrier, total)


def spread(axis, source, target, sems):
    me, size = lax.axis_index(axis), lax.axis_size(axis)
    copies = []
    for k in range(1, size):
        peer = lax.rem(me + k, size)
        copy = pltpu.make_async_remote_copy(
            src_ref=source(peer), dst_ref=target(me),
            send_sem=sems.at[0, k - 1], recv_sem=sems.at[1, k - 1],
            device_id={axis: peer}, device_id_type=MESH)
        copy.start()
        copies.append(copy)
    return copies


def wait_all(copies):
    for copy in copies:
        copy.wait()


def program_kernel(n_e, n_f, frames, depth, start, assign, feat_hbm, gain, taps_hbm, out_t, embed_t, scale_row, shift_row,
                   weight, cot_hbm, values, grad_value, grad_embed,
                   feat, past, taps, own, cot, found, lat, tokens,
                   mod, mod_all, gsum, gram_all, part, landed, quarter, full, rows_out, rows_in, weight_rows,
                   left, staged, qsend, qland, qsum, qall, rsend, rland, vsend, vland, gsend, gland,
                   load_sems, out_sems, halo_sems, mod_sems, gram_sems, part_sems, full_sems, row_sems,
                   lat_sems, q_sems, r_sems, qa_sems, v_sems, g_sems):
    e, f = lax.axis_index("enc"), lax.axis_index("fsdp")
    clips, _, pixels, channels = feat.shape
    width, rows = embed_t.shape
    cols = own.shape[2]
    block = rows // n_e
    slim = width // n_e
    each = pixels // 4
    mine = pl.ds(pl.multiple_of(e * cols, 128), cols)
    loads = [pltpu.make_async_copy(src, dst, load_sems.at[i]) for i, (src, dst) in enumerate(
        [(weight.at[:, :, mine], own), (feat_hbm, feat), (taps_hbm, taps), (cot_hbm, cot)])]
    for copy in loads:
        copy.start()
    for s in range(n_f):
        here = slice(s * rows, (s + 1) * rows)
        mod[s] = jnp.concatenate([scale_row[:, here], shift_row[:, here]], axis=0)
    flat = embed_t[...]
    square = dot(flat, flat, ((1,), (1,)))
    total = jnp.sum(flat.astype(F32), axis=1, keepdims=True)
    gsum[...] = jnp.concatenate([square, jnp.broadcast_to(total, (width, width))], axis=1)
    meet(("enc", "fsdp"))

    def halo(c, peer):
        return pltpu.make_async_remote_copy(
            src_ref=feat_hbm.at[c, pl.ds(frames - 2, 2)], dst_ref=past.at[c],
            send_sem=halo_sems.at[0, c], recv_sem=halo_sems.at[1, c],
            device_id={"enc": lax.rem(peer, n_e)}, device_id_type=MESH)

    mod_copies = spread("fsdp", lambda peer: mod.at[peer], lambda me: mod_all.at[me], mod_sems)
    gram_copies = spread("fsdp", lambda peer: gsum, lambda me: gram_all.at[me], gram_sems)

    @pl.when(e < n_e - 1)
    def _():
        @pl.loop(0, clips)
        def _(c):
            halo(c, e + 1).start()

    @pl.when(e == 0)
    def _():
        past[...] = jnp.zeros_like(past)

    def row_target(k):
        where = n_e * f + k
        return lax.rem(where, n_f), where // n_f

    def row_copy(which, k, slot, target=None):
        src = rows_out.at[k] if which else weight.at[k, :, mine]
        dst = (rows_in if which else weight_rows).at[slot]
        if target is None:
            return pltpu.make_async_copy(src, dst, row_sems.at[0, which, k])
        return pltpu.make_async_remote_copy(
            src_ref=src, dst_ref=dst, send_sem=row_sems.at[0, which, k], recv_sem=row_sems.at[1, which, slot],
            device_id={"fsdp": target}, device_id_type=MESH)

    def send_rows(which):
        for k in range(n_e):
            target, slot = row_target(k)

            @pl.when(target != f)
            def _(k=k, target=target, slot=slot):
                row_copy(which, k, slot, target).start()

            @pl.when(target == f)
            def _(k=k, target=target, slot=slot):
                inside = row_copy(which, k, slot)
                inside.start()
                inside.wait()

    send_rows(0)
    mod_all[f] = mod[f]
    gram_all[f] = gsum[...]
    wait_all(mod_copies)
    wait_all(gram_copies)
    both = jnp.sum(gram_all[...], axis=0) * (1.0 / depth)
    mean = both[:, width:]
    diagonal = (lax.broadcasted_iota(jnp.int32, mean.shape, 0) == lax.broadcasted_iota(jnp.int32, mean.shape, 1))
    gram = both[:, :width] - mean * jnp.sum(mean * diagonal.astype(F32), axis=0, keepdims=True)
    mean = mean[:, :1]
    unit_id = diagonal.astype(BF16)
    centred = flat.astype(F32) - mean
    loads[0].wait()
    own_flat = own[...].astype(F32).reshape(rows, cols).astype(BF16)
    row_id = lax.broadcasted_iota(jnp.int32, (TAIL, rows), 0)
    for s in range(n_f):
        scale = 1.0 + mod_all[s, 0:1, :]
        tail = jnp.where(row_id == 0, scale, jnp.where(row_id == 1, mod_all[s, 1:2, :], 0.0))
        factor = jnp.concatenate([centred * scale, tail], axis=0).astype(BF16)
        part[s] = dot(factor, own_flat).astype(BF16)
    part_copies = spread("fsdp", lambda peer: part.at[peer], lambda me: landed.at[me], part_sems)
    landed[f] = part[f]
    stack = [flat.astype(F32)] + [mod_all[s, 0:1, :] for s in range(n_f)] + [mod_all[s, 1:2, :] for s in range(n_f)]
    spare = rows_out.shape[2] - width - 2 * n_f
    if spare:
        stack.append(jnp.zeros((spare, rows), F32))
    rows_out[...] = jnp.concatenate(stack, axis=0).T.reshape(rows_out.shape)
    send_rows(1)

    gains = gain[0:1, :]
    base = e * frames
    row = lax.broadcasted_iota(jnp.int32, (pixels, width), 0)
    col = lax.broadcasted_iota(jnp.int32, (pixels, width), 1)
    keep = lax.rem(row, 4) == col // (width // 4)
    pick = (lax.broadcasted_iota(jnp.int32, (each, pixels), 0)
            == lax.broadcasted_iota(jnp.int32, (each, pixels), 1) // 4).astype(BF16)
    out_wide = jnp.concatenate([out_t[...]] * 4, axis=0)

    def encode(c, _):
        clip_start = start[c]

        @pl.when(e > 0)
        def _():
            halo(c, e + n_e - 1).wait_recv()

        def norm(frame, frame_id):
            value = frame.astype(F32)
            live = jnp.where((frame_id >= clip_start) & (frame_id >= 0), 1.0, 0.0)
            scaling = lax.rsqrt(jnp.mean(value * value, axis=-1, keepdims=True) + 1e-06) * live
            return (value * scaling * gains).astype(BF16)

        normed = [norm(past[c, i], base - 2 + i) for i in range(2)]
        normed += [norm(feat[c, i], base + i) for i in range(frames)]
        window = jnp.concatenate([jnp.concatenate(normed[i:i + 3], axis=1) for i in range(frames)], axis=0)
        convolved = dot(window, taps[...])
        activation = jnp.concatenate([feat[c, i] for i in range(frames)], axis=0).astype(F32)
        stored = (activation + convolved / (1.0 + jnp.exp(-convolved))).astype(BF16)
        latent = dot(stored, out_wide, ((1,), (1,)))
        picked = []
        for i in range(frames):
            live = jnp.where(base + i >= clip_start, 1.0, 0.0)
            picked.append(dot(pick, jnp.where(keep, latent[i * pixels:(i + 1) * pixels] * live, 0.0).astype(BF16)))
        found[c] = jnp.concatenate(picked, axis=0).astype(BF16)
        return 0

    loads[1].wait()
    loads[2].wait()
    cut = clips // 2
    lax.fori_loop(0, cut, encode, 0)
    wait_all(part_copies)
    quarter[...] = jnp.sum(landed[...].astype(F32), axis=0).astype(BF16)
    full_copies = spread("enc", lambda peer: quarter, lambda me: full.at[me], full_sems)
    full[e] = quarter[...]
    for which in range(2):
        for k in range(n_e):
            target, slot = row_target(k)

            @pl.when(target != f)
            def _(which=which, k=k, target=target, slot=slot):
                row_copy(which, k, slot, target).wait_send()

        for slot in range(n_e):
            origin = (n_f * slot + f) // n_e

            @pl.when(origin != f)
            def _(which=which, slot=slot, origin=origin):
                row_copy(which, slot, slot, origin).wait_recv()

    turned_in = rows_in[...].reshape(rows, rows_in.shape[2]).T
    weight_flat = weight_rows[...].astype(F32).reshape(rows, cols).astype(BF16)
    centred = turned_in[:width] - mean
    for s in range(n_f):
        tail = jnp.where(row_id == 0, turned_in[width + n_f + s:width + n_f + s + 1], 0.0)
        left[s] = jnp.concatenate([centred * (1.0 + turned_in[width + s:width + s + 1]), tail], axis=0).astype(BF16)
    lax.fori_loop(cut, clips, encode, 0)
    for s in range(n_f):
        lat[s] = found[assign[s]]
    lat_copies = spread("fsdp", lambda peer: lat.at[peer], lambda me: tokens.at[me], lat_sems)
    tokens[f] = lat[f]
    wait_all(full_copies)
    loads[3].wait()
    wait_all(lat_copies)
    came = tokens[...].astype(F32)
    flat = jnp.concatenate(
        [came[:, i * each:(i + 1) * each, :].reshape(n_f * each, width) for i in range(frames)], axis=0)
    low = flat.astype(BF16)
    var = jnp.sum(flat * dot(flat, gram, precision=HIGH), axis=1, keepdims=True)
    inv_std = lax.rsqrt(jnp.maximum(var, 0.0) + 1e-06)
    scaled = flat * inv_std
    count = flat.shape[0]
    ones = (lax.broadcasted_iota(jnp.int32, (count, width), 1) == 0).astype(F32)
    wide = jnp.concatenate([scaled, ones], axis=1).astype(BF16)
    dots = jnp.zeros((count, 1), F32)
    out_copies = []
    q_copies = []
    for k in range(1, n_e + 1):
        peer = lax.rem(e + k, n_e)
        here = pl.ds(pl.multiple_of(peer * cols, 128), cols)
        factor = full[peer]
        cot_part = cot[:, here]
        qsend[k - 1] = dot(wide, cot_part, ((0,), (0,)))[:width + TAIL].astype(BF16)
        if k < n_e:
            q_copies.append(pltpu.make_async_remote_copy(
                src_ref=qsend.at[k - 1], dst_ref=qland.at[e],
                send_sem=q_sems.at[0, k - 1], recv_sem=q_sems.at[1, k - 1],
                device_id={"enc": peer}, device_id_type=MESH))
            q_copies[-1].start()
        product = dot(low, factor[:width]) * inv_std
        staged[k - 1] = (product + factor[width:width + TAIL].astype(F32)[1:2]).astype(BF16)
        out_copies.append(pltpu.make_async_copy(staged.at[k - 1], values.at[:, here], out_sems.at[k - 1]))
        out_copies[-1].start()
        dots += jnp.sum(product * cot_part.astype(F32), axis=1, keepdims=True)
    weighted = scaled * (inv_std * dots * (1.0 / depth))
    pairs = dot(weighted.astype(BF16), low, ((0,), (0,)))
    pairs = jnp.concatenate([pairs, jnp.zeros((width, width), F32)], axis=1)
    for i in range(n_e):
        rsend[i] = pairs[i * slim:(i + 1) * slim]
    r_copies = spread("enc", lambda peer: rsend.at[peer], lambda me: rland.at[me], r_sems)
    qland[e] = qsend[n_e - 1]
    rland[e] = rsend[e]
    wait_all(q_copies)
    summed = jnp.sum(qland[...].astype(F32), axis=0)
    low_sum = summed[:width].astype(BF16)
    ends = full[e][width:width + TAIL]
    drift = dot(ends, low_sum, ((1,), (1,)))[:8] * (1.0 / depth)
    drift = jnp.where(lax.broadcasted_iota(jnp.int32, drift.shape, 0) == 0, drift, 0.0)
    wait_all(r_copies)
    head = jnp.sum(rland[...], axis=0)
    extra = [head[i:i + 8] for i in range(0, slim, 8)] + [jnp.concatenate([drift, jnp.zeros_like(drift)], axis=1)]
    if cols > len(extra) * 2 * width:
        extra.append(jnp.zeros((8, cols - len(extra) * 2 * width), F32))
    mixed_sum = jnp.concatenate([summed[:width + 8], jnp.concatenate(extra, axis=1)], axis=0).astype(BF16)
    qsum[...] = mixed_sum
    half_ring = n_f // 2
    partner = f + 1 - 2 * lax.rem(f, 2)

    def onward(src, origin, peer, index):
        copy = pltpu.make_async_remote_copy(
            src_ref=src, dst_ref=qall.at[origin], send_sem=qa_sems.at[0, index], recv_sem=qa_sems.at[1, index],
            device_id={"fsdp": peer}, device_id_type=MESH)
        copy.start()
        return copy

    straight = [onward(qsum, f, lax.rem(f + 2 * j, n_f), j - 1) for j in range(1, half_ring)]
    handed = [onward(qsum, f, partner, half_ring - 1)]
    qall[f] = mixed_sum
    for j in range(1, half_ring):
        straight[j - 1].wait_recv()
        origin = lax.rem(f + n_f - 2 * j, n_f)
        handed.append(onward(qall.at[origin], origin, partner, half_ring - 1 + j))
    for copy in straight:
        copy.wait_send()
    wait_all(handed)
    every = qall[...].reshape(n_f * (width + TAIL), cols)
    lefts = left[...].reshape(n_f * (width + TAIL), rows)
    gradient = dot(lefts, every, ((0,), (0,)))
    for i in range(n_e):
        vsend[i] = gradient[i * block:(i + 1) * block].astype(BF16)
    v_copies = spread("enc", lambda peer: vsend.at[peer], lambda me: vland.at[me], v_sems)
    vland[e] = vsend[e]
    back = dot(every, weight_flat, ((1,), (1,)))
    total = jnp.zeros((width, rows), F32)
    for s in range(n_f):
        start = s * (width + TAIL)
        total += back[start:start + width] * (1.0 + turned_in[width + s:width + s + 1])
    corner = sum(qall[s, width:width + TAIL].astype(F32)[8:] for s in range(n_f))
    fix = jnp.concatenate([corner[:, i * 2 * width:i * 2 * width + width] for i in range(slim // 8 + 1)], axis=0)
    chosen = (lax.broadcasted_iota(jnp.int32, (slim + 8, width), 1)
              == lax.broadcasted_iota(jnp.int32, (slim + 8, width), 0) + e * slim) & (
                  lax.broadcasted_iota(jnp.int32, (slim + 8, width), 0) < slim)
    against = dot(chosen.astype(F32), centred, precision=HIGH)
    against = jnp.where(lax.broadcasted_iota(jnp.int32, against.shape, 0) == slim, 1.0, against)
    total -= dot(fix, against, ((0,), (0,)), precision=HIGH)
    turned = dot(total.astype(BF16), unit_id, ((0,), (0,)))
    turned = jnp.concatenate([turned, jnp.zeros_like(turned)], axis=1).astype(BF16)
    for i in range(n_e):
        gsend[i] = turned[i * block:(i + 1) * block]
    g_copies = spread("enc", lambda peer: gsend.at[peer], lambda me: gland.at[me], g_sems)
    gland[e] = gsend[e]
    wait_all(v_copies)
    for i in range(n_e):
        grad_value[:, i * cols:(i + 1) * cols] = vland[i].astype(F32)
    wait_all(g_copies)
    grad_embed[...] = jnp.sum(gland[...].astype(F32), axis=0)[:, :width]
    wait_all(out_copies)

    @pl.when(e < n_e - 1)
    def _():
        @pl.loop(0, clips)
        def _(c):
            halo(c, e + 1).wait_send()


def local(
    n_e,
    n_f,
    enc_features,
    enc_gain,
    enc_kernel,
    out_kernel,
    clip_start,
    assign,
    embed_weight,
    mod_shift,
    mod_scale,
    value_weight,
    value_cotangent,
):
    clips, frames, pixels, channels = enc_features.shape
    rows, half = value_weight.shape
    width = embed_weight.shape[1]
    depth, cols, block = rows * n_f, half // n_e, rows // n_e
    size = width + TAIL
    slim = width // n_e
    count = frames * value_cotangent.shape[2]
    lanes = -(-(width + 2 * n_f) // 128) * 128
    shape = jax.ShapeDtypeStruct
    dma = lambda *n: pltpu.SemaphoreType.DMA(n)
    b16 = lambda *n: pltpu.VMEM(n, BF16)
    f32 = lambda *n: pltpu.VMEM(n, F32)
    scalars = pl.BlockSpec(memory_space=pltpu.SMEM)
    far = pl.BlockSpec(memory_space=pl.ANY)
    patches = frames * pixels // 4
    values, grad_value, grad_embed = pl.pallas_call(
        functools.partial(program_kernel, n_e, n_f, frames, depth),
        out_shape=(shape((count, half), BF16), shape((block, half), F32), shape((block, width), F32)),
        in_specs=[scalars, scalars, far, VMEM, far, VMEM, VMEM, VMEM, VMEM, far, far],
        out_specs=(far, VMEM, VMEM),
        scratch_shapes=[
            b16(clips, frames, pixels, channels), b16(clips, 2, pixels, channels), b16(3 * channels, channels),
            b16(n_e, block, cols), b16(count, half), b16(clips, patches, width), b16(n_f, patches, width),
            b16(n_f, patches, width),
            f32(n_f, 2, rows), f32(n_f, 2, rows), f32(width, 2 * width), f32(n_f, width, 2 * width),
            b16(n_f, size, cols), b16(n_f, size, cols), b16(size, cols), b16(n_e, size, cols),
            f32(n_e, block, lanes), f32(n_e, block, lanes), b16(n_e, block, cols),
            b16(n_f, size, rows), b16(n_e, count, cols),
            b16(n_e, size, cols), b16(n_e, size, cols), b16(size, cols), b16(n_f, size, cols),
            f32(n_e, slim, 2 * width), f32(n_e, slim, 2 * width),
            b16(n_e, block, cols), b16(n_e, block, cols), b16(n_e, block, 2 * width), b16(n_e, block, 2 * width),
            dma(4), dma(n_e), dma(2, clips), dma(2, n_f - 1), dma(2, n_f - 1), dma(2, n_f - 1), dma(2, n_e - 1),
            dma(2, 2, n_e),
            dma(2, n_f - 1), dma(2, n_e - 1), dma(2, n_e - 1), dma(2, n_f - 1),
            dma(2, n_e - 1), dma(2, n_e - 1)],
        compiler_params=pltpu.CompilerParams(
            collective_id=0, has_side_effects=True, vmem_limit_bytes=56 * 1024 * 1024),
        name="program",
    )(clip_start, assign, enc_features, enc_gain, enc_kernel.reshape(3 * channels, channels), out_kernel.T,
      embed_weight.T, mod_scale, mod_shift, value_weight.reshape(n_e, block, half), value_cotangent.reshape(count, half))
    return (values.reshape(value_cotangent.shape), grad_value, grad_embed)


def solution(mesh):
    in_specs = (
        P(None, "enc", "fsdp", None),
        P(),
        P(),
        P(),
        P(),
        P(),
        P("fsdp", None),
        P("fsdp", None),
        P("fsdp", None),
        P("fsdp", None),
        P("fsdp", "enc", None, None),
    )
    out_specs = (P("fsdp", "enc", None, None), P(("enc", "fsdp"), None), P(("enc", "fsdp"), None))
    body = functools.partial(local, mesh.shape["enc"], mesh.shape["fsdp"])
    return jax.shard_map(body, mesh=mesh, in_specs=in_specs, out_specs=out_specs, check_vma=False)
```

```python
import functools

import jax
import jax.numpy as jnp
from jax import lax
from jax.experimental import pallas as pl
from jax.experimental.pallas import tpu as pltpu
from jax.sharding import PartitionSpec as P

MESH = pl.DeviceIdType.MESH
F32, BF16 = jnp.float32, jnp.bfloat16
HIGH = lax.Precision.HIGHEST
VMEM = pl.BlockSpec(memory_space=pltpu.VMEM)
TAIL = 16


def dot(a, b, dims=((1,), (0,)), precision=None):
    return lax.dot_general(a, b, (dims, ((), ())), preferred_element_type=F32, precision=precision)


def meet(axes):
    barrier = pltpu.get_barrier_semaphore()
    total = 0
    for axis in axes:
        me, size = lax.axis_index(axis), lax.axis_size(axis)
        for k in range(1, size):
            pl.semaphore_signal(barrier, inc=1, device_id={axis: lax.rem(me + k, size)}, device_id_type=MESH)
        total += size - 1
    return barrier, total


def spread(axis, source, target, sems):
    me, size = lax.axis_index(axis), lax.axis_size(axis)
    copies = []
    for k in range(1, size):
        peer = lax.rem(me + k, size)
        copy = pltpu.make_async_remote_copy(
            src_ref=source(peer), dst_ref=target(me),
            send_sem=sems.at[0, k - 1], recv_sem=sems.at[1, k - 1],
            device_id={axis: peer}, device_id_type=MESH)
        copy.start()
        copies.append(copy)
    return copies


def wait_all(copies):
    for copy in copies:
        copy.wait()


def program_kernel(n_e, n_f, frames, depth, start, assign, feat_hbm, gain, taps_hbm, out_t, embed_t, scale_row, shift_row,
                   weight, cot_hbm, values, grad_value, grad_embed,
                   feat, past, taps, own, cot, found, lat, tokens,
                   mod, mod_all, gsum, gram_all, part, landed, quarter, full, rows_out, rows_in, weight_rows,
                   left, staged, qsend, qland, qsum, qall, rsend, rland, vsend, vland, gsend, gland,
                   load_sems, out_sems, halo_sems, mod_sems, gram_sems, part_sems, full_sems, row_sems,
                   lat_sems, q_sems, r_sems, qa_sems, v_sems, g_sems):
    e, f = lax.axis_index("enc"), lax.axis_index("fsdp")
    clips, _, pixels, channels = feat.shape
    width, rows = embed_t.shape
    cols = own.shape[2]
    block = rows // n_e
    slim = width // n_e
    each = pixels // 4
    mine = pl.ds(pl.multiple_of(e * cols, 128), cols)
    barrier, arrivals = meet(("enc", "fsdp"))
    loads = [pltpu.make_async_copy(src, dst, load_sems.at[i]) for i, (src, dst) in enumerate(
        [(weight.at[:, :, mine], own), (feat_hbm, feat), (taps_hbm, taps), (cot_hbm, cot)])]
    for copy in loads:
        copy.start()
    for s in range(n_f):
        here = slice(s * rows, (s + 1) * rows)
        mod[s] = jnp.concatenate([scale_row[:, here], shift_row[:, here]], axis=0)
    flat = embed_t[...]
    square = dot(flat, flat, ((1,), (1,)))
    total = jnp.sum(flat.astype(F32), axis=1, keepdims=True)
    gsum[...] = jnp.concatenate([square, jnp.broadcast_to(total, (width, width))], axis=1)
    pl.semaphore_wait(barrier, arrivals)

    def halo(c, peer):
        return pltpu.make_async_remote_copy(
            src_ref=feat_hbm.at[c, pl.ds(frames - 2, 2)], dst_ref=past.at[c],
            send_sem=halo_sems.at[0, c], recv_sem=halo_sems.at[1, c],
            device_id={"enc": lax.rem(peer, n_e)}, device_id_type=MESH)

    mod_copies = spread("fsdp", lambda peer: mod.at[peer], lambda me: mod_all.at[me], mod_sems)
    gram_copies = spread("fsdp", lambda peer: gsum, lambda me: gram_all.at[me], gram_sems)

    @pl.when(e < n_e - 1)
    def _():
        @pl.loop(0, clips)
        def _(c):
            halo(c, e + 1).start()

    @pl.when(e == 0)
    def _():
        past[...] = jnp.zeros_like(past)

    def row_target(k):
        where = n_e * f + k
        return lax.rem(where, n_f), where // n_f

    def row_copy(which, k, slot, target=None):
        src = rows_out.at[k] if which else weight.at[k, :, mine]
        dst = (rows_in if which else weight_rows).at[slot]
        if target is None:
            return pltpu.make_async_copy(src, dst, row_sems.at[0, which, k])
        return pltpu.make_async_remote_copy(
            src_ref=src, dst_ref=dst, send_sem=row_sems.at[0, which, k], recv_sem=row_sems.at[1, which, slot],
            device_id={"fsdp": target}, device_id_type=MESH)

    def send_rows(which):
        for k in range(n_e):
            target, slot = row_target(k)

            @pl.when(target != f)
            def _(k=k, target=target, slot=slot):
                row_copy(which, k, slot, target).start()

            @pl.when(target == f)
            def _(k=k, target=target, slot=slot):
                inside = row_copy(which, k, slot)
                inside.start()
                inside.wait()

    send_rows(0)
    mod_all[f] = mod[f]
    gram_all[f] = gsum[...]
    wait_all(mod_copies)
    wait_all(gram_copies)
    both = jnp.sum(gram_all[...], axis=0) * (1.0 / depth)
    mean = both[:, width:]
    diagonal = (lax.broadcasted_iota(jnp.int32, mean.shape, 0) == lax.broadcasted_iota(jnp.int32, mean.shape, 1))
    gram = both[:, :width] - mean * jnp.sum(mean * diagonal.astype(F32), axis=0, keepdims=True)
    mean = mean[:, :1]
    unit_id = diagonal.astype(BF16)
    centred = flat.astype(F32) - mean
    loads[0].wait()
    own_flat = own[...].astype(F32).reshape(rows, cols).astype(BF16)
    row_id = lax.broadcasted_iota(jnp.int32, (TAIL, rows), 0)
    for s in range(n_f):
        scale = 1.0 + mod_all[s, 0:1, :]
        tail = jnp.where(row_id == 0, scale, jnp.where(row_id == 1, mod_all[s, 1:2, :], 0.0))
        factor = jnp.concatenate([centred * scale, tail], axis=0).astype(BF16)
        part[s] = dot(factor, own_flat).astype(BF16)
    part_copies = spread("fsdp", lambda peer: part.at[peer], lambda me: landed.at[me], part_sems)
    landed[f] = part[f]
    stack = [flat.astype(F32)] + [mod_all[s, 0:1, :] for s in range(n_f)] + [mod_all[s, 1:2, :] for s in range(n_f)]
    spare = rows_out.shape[2] - width - 2 * n_f
    if spare:
        stack.append(jnp.zeros((spare, rows), F32))
    rows_out[...] = jnp.concatenate(stack, axis=0).T.reshape(rows_out.shape)
    send_rows(1)

    gains = gain[0:1, :]
    base = e * frames
    row = lax.broadcasted_iota(jnp.int32, (pixels, width), 0)
    col = lax.broadcasted_iota(jnp.int32, (pixels, width), 1)
    keep = lax.rem(row, 4) == col // (width // 4)
    pick = (lax.broadcasted_iota(jnp.int32, (each, pixels), 0)
            == lax.broadcasted_iota(jnp.int32, (each, pixels), 1) // 4).astype(BF16)
    out_wide = jnp.concatenate([out_t[...]] * 4, axis=0)

    def encode(c, _):
        clip_start = start[c]

        @pl.when(e > 0)
        def _():
            halo(c, e + n_e - 1).wait_recv()

        def norm(frame, frame_id):
            value = frame.astype(F32)
            live = jnp.where((frame_id >= clip_start) & (frame_id >= 0), 1.0, 0.0)
            scaling = lax.rsqrt(jnp.mean(value * value, axis=-1, keepdims=True) + 1e-06) * live
            return (value * scaling * gains).astype(BF16)

        normed = [norm(past[c, i], base - 2 + i) for i in range(2)]
        normed += [norm(feat[c, i], base + i) for i in range(frames)]
        window = jnp.concatenate([jnp.concatenate(normed[i:i + 3], axis=1) for i in range(frames)], axis=0)
        convolved = dot(window, taps[...])
        activation = jnp.concatenate([feat[c, i] for i in range(frames)], axis=0).astype(F32)
        stored = (activation + convolved / (1.0 + jnp.exp(-convolved))).astype(BF16)
        latent = dot(stored, out_wide, ((1,), (1,)))
        picked = []
        for i in range(frames):
            live = jnp.where(base + i >= clip_start, 1.0, 0.0)
            picked.append(dot(pick, jnp.where(keep, latent[i * pixels:(i + 1) * pixels] * live, 0.0).astype(BF16)))
        found[c] = jnp.concatenate(picked, axis=0).astype(BF16)
        return 0

    loads[1].wait()
    loads[2].wait()
    cut = clips // 2
    lax.fori_loop(0, cut, encode, 0)
    wait_all(part_copies)
    quarter[...] = jnp.sum(landed[...].astype(F32), axis=0).astype(BF16)
    full_copies = spread("enc", lambda peer: quarter, lambda me: full.at[me], full_sems)
    full[e] = quarter[...]
    for which in range(2):
        for k in range(n_e):
            target, slot = row_target(k)

            @pl.when(target != f)
            def _(which=which, k=k, target=target, slot=slot):
                row_copy(which, k, slot, target).wait_send()

        for slot in range(n_e):
            origin = (n_f * slot + f) // n_e

            @pl.when(origin != f)
            def _(which=which, slot=slot, origin=origin):
                row_copy(which, slot, slot, origin).wait_recv()

    turned_in = rows_in[...].reshape(rows, rows_in.shape[2]).T
    weight_flat = weight_rows[...].astype(F32).reshape(rows, cols).astype(BF16)
    centred = turned_in[:width] - mean
    for s in range(n_f):
        tail = jnp.where(row_id == 0, turned_in[width + n_f + s:width + n_f + s + 1], 0.0)
        left[s] = jnp.concatenate([centred * (1.0 + turned_in[width + s:width + s + 1]), tail], axis=0).astype(BF16)
    lax.fori_loop(cut, clips, encode, 0)
    for s in range(n_f):
        lat[s] = found[assign[s]]
    lat_copies = spread("fsdp", lambda peer: lat.at[peer], lambda me: tokens.at[me], lat_sems)
    tokens[f] = lat[f]
    wait_all(full_copies)
    loads[3].wait()
    wait_all(lat_copies)
    came = tokens[...].astype(F32)
    flat = jnp.concatenate(
        [came[:, i * each:(i + 1) * each, :].reshape(n_f * each, width) for i in range(frames)], axis=0)
    low = flat.astype(BF16)
    var = jnp.sum(flat * dot(flat, gram, precision=HIGH), axis=1, keepdims=True)
    inv_std = lax.rsqrt(jnp.maximum(var, 0.0) + 1e-06)
    scaled = flat * inv_std
    count = flat.shape[0]
    ones = (lax.broadcasted_iota(jnp.int32, (count, width), 1) == 0).astype(F32)
    wide = jnp.concatenate([scaled, ones], axis=1).astype(BF16)
    dots = jnp.zeros((count, 1), F32)
    out_copies = []
    q_copies = []
    for k in range(1, n_e + 1):
        peer = lax.rem(e + k, n_e)
        here = pl.ds(pl.multiple_of(peer * cols, 128), cols)
        factor = full[peer]
        cot_part = cot[:, here]
        qsend[k - 1] = dot(wide, cot_part, ((0,), (0,)))[:width + TAIL].astype(BF16)
        if k < n_e:
            q_copies.append(pltpu.make_async_remote_copy(
                src_ref=qsend.at[k - 1], dst_ref=qland.at[e],
                send_sem=q_sems.at[0, k - 1], recv_sem=q_sems.at[1, k - 1],
                device_id={"enc": peer}, device_id_type=MESH))
            q_copies[-1].start()
        product = dot(low, factor[:width]) * inv_std
        staged[k - 1] = (product + factor[width:width + TAIL].astype(F32)[1:2]).astype(BF16)
        out_copies.append(pltpu.make_async_copy(staged.at[k - 1], values.at[:, here], out_sems.at[k - 1]))
        out_copies[-1].start()
        dots += jnp.sum(product * cot_part.astype(F32), axis=1, keepdims=True)
    weighted = scaled * (inv_std * dots * (1.0 / depth))
    pairs = dot(weighted.astype(BF16), low, ((0,), (0,)))
    pairs = jnp.concatenate([pairs, jnp.zeros((width, width), F32)], axis=1)
    for i in range(n_e):
        rsend[i] = pairs[i * slim:(i + 1) * slim]
    r_copies = spread("enc", lambda peer: rsend.at[peer], lambda me: rland.at[me], r_sems)
    qland[e] = qsend[n_e - 1]
    rland[e] = rsend[e]
    wait_all(q_copies)
    summed = jnp.sum(qland[...].astype(F32), axis=0)
    low_sum = summed[:width].astype(BF16)
    ends = full[e][width:width + TAIL]
    drift = dot(ends, low_sum, ((1,), (1,)))[:8] * (1.0 / depth)
    drift = jnp.where(lax.broadcasted_iota(jnp.int32, drift.shape, 0) == 0, drift, 0.0)
    wait_all(r_copies)
    head = jnp.sum(rland[...], axis=0)
    extra = [head[i:i + 8] for i in range(0, slim, 8)] + [jnp.concatenate([drift, jnp.zeros_like(drift)], axis=1)]
    if cols > len(extra) * 2 * width:
        extra.append(jnp.zeros((8, cols - len(extra) * 2 * width), F32))
    mixed_sum = jnp.concatenate([summed[:width + 8], jnp.concatenate(extra, axis=1)], axis=0).astype(BF16)
    qsum[...] = mixed_sum
    half_ring = n_f // 2
    partner = f + 1 - 2 * lax.rem(f, 2)

    def onward(src, origin, peer, index):
        copy = pltpu.make_async_remote_copy(
            src_ref=src, dst_ref=qall.at[origin], send_sem=qa_sems.at[0, index], recv_sem=qa_sems.at[1, index],
            device_id={"fsdp": peer}, device_id_type=MESH)
        copy.start()
        return copy

    straight = [onward(qsum, f, lax.rem(f + 2 * j, n_f), j - 1) for j in range(1, half_ring)]
    handed = [onward(qsum, f, partner, half_ring - 1)]
    qall[f] = mixed_sum
    for j in range(1, half_ring):
        straight[j - 1].wait_recv()
        origin = lax.rem(f + n_f - 2 * j, n_f)
        handed.append(onward(qall.at[origin], origin, partner, half_ring - 1 + j))
    for copy in straight:
        copy.wait_send()
    wait_all(handed)
    every = qall[...].reshape(n_f * (width + TAIL), cols)
    lefts = left[...].reshape(n_f * (width + TAIL), rows)
    gradient = dot(lefts, every, ((0,), (0,)))
    for i in range(n_e):
        vsend[i] = gradient[i * block:(i + 1) * block].astype(BF16)
    v_copies = spread("enc", lambda peer: vsend.at[peer], lambda me: vland.at[me], v_sems)
    vland[e] = vsend[e]
    back = dot(every, weight_flat, ((1,), (1,)))
    total = jnp.zeros((width, rows), F32)
    for s in range(n_f):
        start = s * (width + TAIL)
        total += back[start:start + width] * (1.0 + turned_in[width + s:width + s + 1])
    corner = sum(qall[s, width:width + TAIL].astype(F32)[8:] for s in range(n_f))
    fix = jnp.concatenate([corner[:, i * 2 * width:i * 2 * width + width] for i in range(slim // 8 + 1)], axis=0)
    chosen = (lax.broadcasted_iota(jnp.int32, (slim + 8, width), 1)
              == lax.broadcasted_iota(jnp.int32, (slim + 8, width), 0) + e * slim) & (
                  lax.broadcasted_iota(jnp.int32, (slim + 8, width), 0) < slim)
    against = dot(chosen.astype(F32), centred, precision=HIGH)
    against = jnp.where(lax.broadcasted_iota(jnp.int32, against.shape, 0) == slim, 1.0, against)
    total -= dot(fix, against, ((0,), (0,)), precision=HIGH)
    turned = dot(total.astype(BF16), unit_id, ((0,), (0,)))
    turned = jnp.concatenate([turned, jnp.zeros_like(turned)], axis=1).astype(BF16)
    for i in range(n_e):
        gsend[i] = turned[i * block:(i + 1) * block]
    g_copies = spread("enc", lambda peer: gsend.at[peer], lambda me: gland.at[me], g_sems)
    gland[e] = gsend[e]
    wait_all(v_copies)
    for i in range(n_e):
        grad_value[:, i * cols:(i + 1) * cols] = vland[i].astype(F32)
    wait_all(g_copies)
    grad_embed[...] = dot(diagonal.astype(F32), jnp.sum(gland[...].astype(F32), axis=0)[:, :width], ((1,), (1,)), HIGH)
    wait_all(out_copies)

    @pl.when(e < n_e - 1)
    def _():
        @pl.loop(0, clips)
        def _(c):
            halo(c, e + 1).wait_send()


def local(
    n_e,
    n_f,
    enc_features,
    enc_gain,
    enc_kernel,
    out_kernel,
    clip_start,
    assign,
    embed_weight,
    mod_shift,
    mod_scale,
    value_weight,
    value_cotangent,
):
    clips, frames, pixels, channels = enc_features.shape
    rows, half = value_weight.shape
    width = embed_weight.shape[1]
    depth, cols, block = rows * n_f, half // n_e, rows // n_e
    size = width + TAIL
    slim = width // n_e
    count = frames * value_cotangent.shape[2]
    lanes = -(-(width + 2 * n_f) // 128) * 128
    shape = jax.ShapeDtypeStruct
    dma = lambda *n: pltpu.SemaphoreType.DMA(n)
    b16 = lambda *n: pltpu.VMEM(n, BF16)
    f32 = lambda *n: pltpu.VMEM(n, F32)
    scalars = pl.BlockSpec(memory_space=pltpu.SMEM)
    far = pl.BlockSpec(memory_space=pl.ANY)
    patches = frames * pixels // 4
    values, grad_value, grad_embed = pl.pallas_call(
        functools.partial(program_kernel, n_e, n_f, frames, depth),
        out_shape=(shape((count, half), BF16), shape((block, half), F32), shape((width, block), F32)),
        in_specs=[scalars, scalars, far, VMEM, far, VMEM, VMEM, VMEM, VMEM, far, far],
        out_specs=(far, VMEM, VMEM),
        scratch_shapes=[
            b16(clips, frames, pixels, channels), b16(clips, 2, pixels, channels), b16(3 * channels, channels),
            b16(n_e, block, cols), b16(count, half), b16(clips, patches, width), b16(n_f, patches, width),
            b16(n_f, patches, width),
            f32(n_f, 2, rows), f32(n_f, 2, rows), f32(width, 2 * width), f32(n_f, width, 2 * width),
            b16(n_f, size, cols), b16(n_f, size, cols), b16(size, cols), b16(n_e, size, cols),
            f32(n_e, block, lanes), f32(n_e, block, lanes), b16(n_e, block, cols),
            b16(n_f, size, rows), b16(n_e, count, cols),
            b16(n_e, size, cols), b16(n_e, size, cols), b16(size, cols), b16(n_f, size, cols),
            f32(n_e, slim, 2 * width), f32(n_e, slim, 2 * width),
            b16(n_e, block, cols), b16(n_e, block, cols), b16(n_e, block, 2 * width), b16(n_e, block, 2 * width),
            dma(4), dma(n_e), dma(2, clips), dma(2, n_f - 1), dma(2, n_f - 1), dma(2, n_f - 1), dma(2, n_e - 1),
            dma(2, 2, n_e),
            dma(2, n_f - 1), dma(2, n_e - 1), dma(2, n_e - 1), dma(2, n_f - 1),
            dma(2, n_e - 1), dma(2, n_e - 1)],
        compiler_params=pltpu.CompilerParams(
            collective_id=0, has_side_effects=True, vmem_limit_bytes=56 * 1024 * 1024),
        name="program",
    )(clip_start, assign, enc_features, enc_gain, enc_kernel.reshape(3 * channels, channels), out_kernel.T,
      embed_weight.T, mod_scale, mod_shift, value_weight.reshape(n_e, block, half), value_cotangent.reshape(count, half))
    return (values.reshape(value_cotangent.shape), grad_value, grad_embed.T)


def solution(mesh):
    in_specs = (
        P(None, "enc", "fsdp", None),
        P(),
        P(),
        P(),
        P(),
        P(),
        P("fsdp", None),
        P("fsdp", None),
        P("fsdp", None),
        P("fsdp", None),
        P("fsdp", "enc", None, None),
    )
    out_specs = (P("fsdp", "enc", None, None), P(("enc", "fsdp"), None), P(("enc", "fsdp"), None))
    body = functools.partial(local, mesh.shape["enc"], mesh.shape["fsdp"])
    return jax.shard_map(body, mesh=mesh, in_specs=in_specs, out_specs=out_specs, check_vma=False)
```
